256 devices in a mesh: row: 8 (over z_lo, core), col: 32 (over x, z_hi, y).
Axes of the slice: x: 4, y: 4, z: 8 (z_hi: 2, z_lo: 4; z = z_hi * 4 + z_lo), core: 2. Of those that a mesh axis runs over, the one named last changes fastest.
Arguments:
- alignment: bfloat16 [512, 1024, 256], P('col', 'row'), may hold values from -8 to 8, as said below
- column_mask: int32 [512, 1024], replicated, may hold values from 0 to 1, as said below
- chain_index: int32 [1024], replicated, may hold values from 0 to 3, never falling along the last dimension, each value on 1 to 512 neighbouring positions
- attention_norm_gain: float32 [256], replicated, may hold values from 0.1 to 1.9
- query_weight: bfloat16 [256, 256], replicated, may hold values from -2 to 2
- key_weight: bfloat16 [256, 256], replicated, may hold values from -2 to 2
- value_matrix: bfloat16 [256, 256], replicated, may hold values from -0.375 to 0.375
- gate_matrix: bfloat16 [256, 256], replicated, may hold values from -0.375 to 0.375
- gate_bias: float32 [256], replicated, may hold values from -4 to 4
- attention_output_weight: bfloat16 [256, 256], replicated, may hold values from -0.375 to 0.375
- attention_output_bias: float32 [256], replicated, may hold values from -3 to 3
- outer_norm_gain: float32 [256], replicated, may hold values from 0.1 to 1.9
- left_factor_weight: bfloat16 [256, 32], replicated, may hold values from -0.375 to 0.375
- right_factor_weight: bfloat16 [256, 32], replicated, may hold values from -0.375 to 0.375
- pair_weight: bfloat16 [1024, 128], replicated, may hold values from -0.1875 to 0.1875
- chain_bias: float32 [128], replicated, may hold values from -4 to 4
Outputs:
- updated_alignment: bfloat16 [512, 1024, 256], P(None, ('row', 'col'))
- pair_update: bfloat16 [1024, 1024, 128], P('row', 'col')
The draws below stay inside these ranges and needn't reach their ends.
Inputs may be any that keep to these rules, and one draw needn't show every extreme that they name: `alignment`: aligned features: a per-residue profile shared by all sequences plus per-sequence variation. `column_mask`: row 0 (the query sequence) is 1 at every residue.
All inputs are finite; a program needn't handle non-finite values.
Results may differ from the reference program's by a relative error of at most 0.0089.
Values may be sent and summed in bfloat16 or wider, within the bound.
No kernel may reach another device: no remote copies, remote signals or barrier semaphores. Data moves between devices by JAX's collectives and lax.ppermute only.
A program may use at most 64 MiB of HBM per device.

```python
import math
import jax
import jax.numpy as jnp
import numpy as np
from jax import lax

ALIGN_FEATURES = 256
PAIR_DIM = 128
FACTOR_FEATURES = 32
HEAD_COUNT = 8
HEAD_FEATURES = 32
SEQUENCE_COUNT = 512
RESIDUE_TOTAL = 1024


def shared_base(key):
    return jax.random.normal(jax.random.fold_in(key, 7), (ALIGN_FEATURES, HEAD_COUNT * HEAD_FEATURES), jnp.float32)


def draw_alignment(key, part):
    key = jax.random.fold_in(key, 1)
    profile_random_key, noise_random_key = jax.random.split(key, 2)
    sequence_profile = jax.random.normal(profile_random_key, (1, RESIDUE_TOTAL, ALIGN_FEATURES), jnp.float32)
    random_noise = jax.random.normal(noise_random_key, (SEQUENCE_COUNT, RESIDUE_TOTAL, ALIGN_FEATURES), jnp.float32)
    value_rows = sequence_profile + random_noise
    return jnp.clip(value_rows, -8.0, 8.0).astype(jnp.bfloat16)


def draw_column_mask(key, part):
    key = jax.random.fold_in(key, 2)
    levels = jax.random.randint(key, (SEQUENCE_COUNT, RESIDUE_TOTAL), 0, 5)
    present = (levels > 0).astype(jnp.int32)
    return present.at[0].set(1)


def draw_query_weight(key, part):
    base_alignment = shared_base(key)
    value_rows = base_alignment * ALIGN_FEATURES ** (-0.5)
    return jnp.clip(value_rows, -2.0, 2.0).astype(jnp.bfloat16)


def draw_key_weight(key, part):
    key = jax.random.fold_in(key, 4)
    local_rows = jax.random.normal(key, (ALIGN_FEATURES, HEAD_COUNT * HEAD_FEATURES), jnp.float32)
    value_rows = local_rows * ALIGN_FEATURES ** (-0.5)
    return jnp.clip(value_rows, -2.0, 2.0).astype(jnp.bfloat16)


def length_profile(amount, total, reach, lean):
    portions = [(1 << 20) // math.isqrt(grade ** lean) + 1 for grade in range(2, amount + 1)]
    rest, given = total - reach - (amount - 1), [1] * (amount - 1)
    while rest > 0:
        free = [i for i in range(amount - 1) if given[i] < reach]
        whole, left = sum([portions[i] for i in free]), rest
        for i in free:
            more = min(reach - given[i], max(1, left * portions[i] // whole), rest)
            given[i] = given[i] + more
            rest = rest - more
    return np.array([reach] + given)


def ragged_sizes(rng, number_of, total, limit, slope):
    if number_of == 2:
        one = jax.random.randint(rng, (), max(1, total - limit), min(limit, total - 1) + 1)
        return jnp.stack([one, total - one])
    tallies = jnp.asarray(length_profile(number_of, total, limit, slope), jnp.int32)
    twos = (number_of - 1) // 2
    giver, taker = tallies[1:1 + 2 * twos:2], tallies[2:2 + 2 * twos:2]
    room = jnp.minimum(giver - 1, limit - taker)
    passed = jax.random.randint(jax.random.fold_in(rng, 1), (twos,), 0, 1 << 20) % (room + 1)
    tallies = tallies.at[1:1 + 2 * twos:2].set(giver - passed).at[2:2 + 2 * twos:2].set(taker + passed)
    return tallies[jax.random.permutation(jax.random.fold_in(rng, 2), number_of)]


def scatter_about(key, dims, scale, most, kind=jnp.bfloat16):
    values = jax.random.normal(key, dims, jnp.float32) * scale
    return jnp.minimum(jnp.maximum(values, -most), most).astype(kind)


def setup_inputs(seed: int = 0) -> dict:
    key_list = jax.random.split(jax.random.key(seed), 17)
    return {
        "alignment": draw_alignment(jax.random.fold_in(key_list[16], 71), 0),
        "column_mask": draw_column_mask(jax.random.fold_in(key_list[16], 71), 0),
        "chain_index": jnp.searchsorted(jnp.cumsum(ragged_sizes(key_list[2], 4, RESIDUE_TOTAL, RESIDUE_TOTAL // 2, 1)), jnp.arange(RESIDUE_TOTAL), side="right").astype(jnp.int32),
        "attention_norm_gain": jnp.clip(1.0 + 0.18 * jax.random.normal(key_list[3], (ALIGN_FEATURES,), jnp.float32), 0.1, 1.9),
        "query_weight": draw_query_weight(jax.random.fold_in(key_list[16], 71), 0),
        "key_weight": draw_key_weight(jax.random.fold_in(key_list[16], 71), 0),
        "value_matrix": scatter_about(key_list[6], (ALIGN_FEATURES, HEAD_COUNT * HEAD_FEATURES), ALIGN_FEATURES ** -0.5, 0.375),
        "gate_matrix": scatter_about(key_list[7], (ALIGN_FEATURES, HEAD_COUNT * HEAD_FEATURES), ALIGN_FEATURES ** -0.5, 0.375),
        "gate_bias": scatter_about(key_list[8], (HEAD_COUNT * HEAD_FEATURES,), 1.0, 4.0, jnp.float32),
        "attention_output_weight": scatter_about(key_list[9], (HEAD_COUNT * HEAD_FEATURES, ALIGN_FEATURES), (HEAD_COUNT * HEAD_FEATURES) ** -0.5, 0.375),
        "attention_output_bias": scatter_about(key_list[10], (ALIGN_FEATURES,), 0.5, 3.0, jnp.float32),
        "outer_norm_gain": jnp.clip(1.0 + 0.18 * jax.random.normal(key_list[11], (ALIGN_FEATURES,), jnp.float32), 0.1, 1.9),
        "left_factor_weight": scatter_about(key_list[12], (ALIGN_FEATURES, FACTOR_FEATURES), ALIGN_FEATURES ** -0.5, 0.375),
        "right_factor_weight": scatter_about(key_list[13], (ALIGN_FEATURES, FACTOR_FEATURES), ALIGN_FEATURES ** -0.5, 0.375),
        "pair_weight": scatter_about(key_list[14], (FACTOR_FEATURES * FACTOR_FEATURES, PAIR_DIM), (FACTOR_FEATURES * FACTOR_FEATURES) ** -0.5, 0.1875),
        "chain_bias": scatter_about(key_list[15], (PAIR_DIM,), 1.0, 4.0, jnp.float32),
    }


def layer_normalize(value_rows, gain):
    value_rows = value_rows.astype(jnp.float32)
    average = lax.optimization_barrier(jnp.mean(value_rows, -1, keepdims=True))
    centred = value_rows - average
    variance = lax.optimization_barrier(jnp.mean(centred * centred, -1, keepdims=True))
    return centred * lax.rsqrt(variance + 1e-05) * gain

def column_attention(block_row_count, mask_rows, attention_norm_gain, query_weight, key_weight, value_matrix, gate_matrix, gate_bias, attention_output_weight, attention_output_bias):
    sequence_total, residue_count, alignment_width = block_row_count.shape
    normed_alignment = layer_normalize(block_row_count, attention_norm_gain).astype(jnp.bfloat16).reshape(sequence_total * residue_count, alignment_width)

    def project(weight):
        product = jnp.dot(normed_alignment, weight, preferred_element_type=jnp.float32)
        return product.astype(jnp.bfloat16).reshape(sequence_total, residue_count, HEAD_COUNT, HEAD_FEATURES)
    queries = project(query_weight)
    keys_all = project(key_weight)
    values_all = project(value_matrix)
    gates = jax.nn.sigmoid(jnp.dot(normed_alignment, gate_matrix, preferred_element_type=jnp.float32) + gate_bias)
    gates = gates.reshape(sequence_total, residue_count, HEAD_COUNT * HEAD_FEATURES)

    def attend_one(residue):
        query_col = lax.dynamic_index_in_dim(queries, residue, 1, keepdims=False).astype(jnp.float32)
        key_col = lax.dynamic_index_in_dim(keys_all, residue, 1, keepdims=False).astype(jnp.float32)
        value_col = lax.dynamic_index_in_dim(values_all, residue, 1, keepdims=False).astype(jnp.float32)
        scores = jnp.einsum('shd,thd->hst', query_col, key_col) * HEAD_FEATURES ** (-0.5)
        live = lax.dynamic_index_in_dim(mask_rows, residue, 1, keepdims=False)
        scores = jnp.where(live[None, None, :] > 0, scores, jnp.float32(-1000000000.0))
        weights = jax.nn.softmax(scores, axis=-1).astype(jnp.bfloat16)
        mixed = jnp.einsum('hst,thd->shd', weights.astype(jnp.float32), value_col)
        gate_col = lax.dynamic_index_in_dim(gates, residue, 1, keepdims=False)
        return (mixed.reshape(sequence_total, HEAD_COUNT * HEAD_FEATURES) * gate_col).astype(jnp.bfloat16)
    gated_output = lax.map(attend_one, jnp.arange(residue_count, dtype=jnp.int32))
    gated_output = jnp.swapaxes(gated_output, 0, 1).reshape(sequence_total * residue_count, HEAD_COUNT * HEAD_FEATURES)
    projected_output = jnp.dot(gated_output, attention_output_weight, preferred_element_type=jnp.float32).reshape(sequence_total, residue_count, alignment_width)
    return (projected_output + attention_output_bias + block_row_count.astype(jnp.float32)).astype(jnp.bfloat16)

def pair_rows(left_rows, right_cols, mask_rows, mask_cols, chain_rows, chain_cols, pair_weight, chain_bias):
    row_count = left_rows.shape[1]
    col_count = right_cols.shape[1]
    outer_product = jnp.einsum('sip,sjq->ijpq', left_rows.astype(jnp.float32), right_cols.astype(jnp.float32))
    outer_product = outer_product.astype(jnp.bfloat16).reshape(row_count * col_count, -1)
    projected_output = jnp.dot(outer_product, pair_weight, preferred_element_type=jnp.float32).reshape(row_count, col_count, -1)
    counts = jnp.dot(mask_rows.astype(jnp.float32).T, mask_cols.astype(jnp.float32), precision=lax.Precision.HIGHEST)
    same_chain = (chain_rows[:, None] == chain_cols[None, :]).astype(jnp.float32)
    result = projected_output / (counts + 0.001)[:, :, None] + same_chain[:, :, None] * chain_bias
    return result.astype(jnp.bfloat16)

def reference(alignment, column_mask, chain_index, attention_norm_gain, query_weight, key_weight, value_matrix, gate_matrix, gate_bias, attention_output_weight, attention_output_bias, outer_norm_gain, left_factor_weight, right_factor_weight, pair_weight, chain_bias):
    sequence_total, residue_total, alignment_width = alignment.shape
    block_size = 32

    def attend_block(block_index):
        first_row = (block_index * block_size).astype(jnp.int32)
        rows = lax.dynamic_slice_in_dim(alignment, first_row, block_size, 1)
        mask_rows = lax.dynamic_slice_in_dim(column_mask, first_row, block_size, 1)
        return column_attention(rows, mask_rows, attention_norm_gain, query_weight, key_weight, value_matrix, gate_matrix, gate_bias, attention_output_weight, attention_output_bias)
    updated_rows = lax.map(attend_block, jnp.arange(residue_total // block_size, dtype=jnp.int32))
    updated_rows = jnp.moveaxis(updated_rows, 0, 1).reshape(sequence_total, residue_total, alignment_width)
    outer_normed_alignment = layer_normalize(updated_rows, outer_norm_gain).astype(jnp.bfloat16).reshape(sequence_total * residue_total, alignment_width)
    mask_float = column_mask.astype(jnp.float32)[:, :, None]
    left = (jnp.dot(outer_normed_alignment, left_factor_weight, preferred_element_type=jnp.float32).reshape(sequence_total, residue_total, -1) * mask_float).astype(jnp.bfloat16)
    right = (jnp.dot(outer_normed_alignment, right_factor_weight, preferred_element_type=jnp.float32).reshape(sequence_total, residue_total, -1) * mask_float).astype(jnp.bfloat16)
    pair_block = 16

    def pair_block_rows(block_index):
        first_row = (block_index * pair_block).astype(jnp.int32)
        left_rows = lax.dynamic_slice_in_dim(left, first_row, pair_block, 1)
        mask_rows = lax.dynamic_slice_in_dim(column_mask, first_row, pair_block, 1)
        chain_rows = lax.dynamic_slice_in_dim(chain_index, first_row, pair_block, 0)
        return pair_rows(left_rows, right, mask_rows, column_mask, chain_rows, chain_index, pair_weight, chain_bias)
    pair_update = lax.map(pair_block_rows, jnp.arange(residue_total // pair_block, dtype=jnp.int32))
    pair_update = pair_update.reshape(residue_total, residue_total, -1)
    return (updated_rows, pair_update)
```

```python
import functools
import math

import jax
import jax.numpy as jnp
import numpy as np
from jax import lax
from jax.experimental import pallas as pl
from jax.experimental.pallas import tpu as pltpu
from jax.sharding import PartitionSpec as P

HEAD_COUNT = 8
HEAD_FEATURES = 32
NT = (((1,), (1,)), ((), ()))
F32, BF16 = jnp.float32, jnp.bfloat16
SB = 128

def norm_rows(x, gain):
    average = jnp.mean(x, -1, keepdims=True)
    centred = x - average
    variance = jnp.mean(centred * centred, -1, keepdims=True)
    return centred * lax.rsqrt(variance + 1e-05) * gain

def dot(a, b):
    return jnp.dot(a, b, preferred_element_type=F32)

def dot_nt(a, b):
    return lax.dot_general(a, b, NT, preferred_element_type=F32)

def attend_kernel(x_ref, kbias_ref, mask_ref, gain1_ref, wqkvg_ref, gbias_ref, wo_ref, obias_ref, gain2_ref, wlr_ref,
                  up_ref, left_ref, right_ref, qa_ref, ka_ref, va_ref, gated_ref):
    rows, width = qa_ref.shape[1], x_ref.shape[-1]
    x = x_ref[...].reshape(rows, width).astype(F32)
    normed = norm_rows(x, gain1_ref[...]).astype(BF16)
    scale = math.log2(math.e) * HEAD_FEATURES ** (-0.5)
    lane = lax.broadcasted_iota(jnp.int32, (1, 128), 1)
    first = jnp.broadcast_to(jnp.where(lane == 0, 1.0, 0.0).astype(BF16), (rows, 128))
    kbias = kbias_ref[...].reshape(rows, 128)
    queries = (dot(normed, wqkvg_ref[:, 0:256]) * scale).astype(BF16)
    keys = dot(normed, wqkvg_ref[:, 256:512]).astype(BF16)
    values = dot(normed, wqkvg_ref[:, 512:768]).astype(BF16)
    for g in range(2):
        qa_ref[g] = jnp.concatenate([queries[:, g * 128:(g + 1) * 128], first], axis=1)
        for h in range(4):
            on = (lane // 32 == h)
            kept = jnp.where(on, 1.0, 0.0).astype(BF16)
            ka_ref[g * 4 + h] = jnp.concatenate([keys[:, g * 128:(g + 1) * 128] * kept, kbias], axis=1)
            va_ref[g, h * rows:(h + 1) * rows, :] = jnp.concatenate(
                [values[:, g * 128:(g + 1) * 128] * kept, jnp.broadcast_to(kept, (rows, 128))], axis=1)
    gates = jax.nn.sigmoid(dot(normed, wqkvg_ref[:, 768:1024]) + gbias_ref[...])
    gated_ref[...] = gates
    for g in range(2):
        for b in range(rows // SB):
            q = qa_ref[g, b * SB:(b + 1) * SB, :]
            total = None
            for h in range(4):
                s = dot_nt(q, ka_ref[g * 4 + h])
                m = jnp.max(s, axis=-1, keepdims=True)
                p = jnp.exp2(s - m).astype(BF16)
                part = dot(p, va_ref[g, h * rows:(h + 1) * rows, :])
                total = part if total is None else total + part
            out = total[:, :128] / total[:, 128:]
            sl = (slice(b * SB, (b + 1) * SB), slice(g * 128, (g + 1) * 128))
            gated_ref[sl] = gated_ref[sl] * out
    gated = gated_ref[...].astype(BF16)
    updated = (dot(gated, wo_ref[...]) + obias_ref[...] + x).astype(BF16)
    up_ref[...] = updated.reshape(up_ref.shape)
    again = norm_rows(updated.astype(F32), gain2_ref[...]).astype(BF16)
    factors = dot_nt(wlr_ref[...], again) * mask_ref[...].reshape(1, rows)
    left_ref[...] = factors[:32].astype(BF16).reshape(left_ref.shape)
    right_ref[...] = factors[32:].astype(BF16).reshape(right_ref.shape)

def attend(x, kbias, mask, gain1, wqkvg, gbias, wo, obias, gain2, wlr_t):
    groups, count, per, width = x.shape
    rows = groups * per
    whole = lambda a: pl.BlockSpec(a.shape, lambda k: (0,) * a.ndim)
    return pl.pallas_call(
        attend_kernel,
        grid=(count,),
        in_specs=[
            pl.BlockSpec((groups, 1, per, width), lambda k: (0, k, 0, 0)),
            pl.BlockSpec((1, rows, 128), lambda k: (k, 0, 0)),
            pl.BlockSpec((1, 1, rows), lambda k: (k, 0, 0)),
            whole(gain1), whole(wqkvg), whole(gbias), whole(wo), whole(obias), whole(gain2), whole(wlr_t),
        ],
        out_specs=[
            pl.BlockSpec((1, rows, width), lambda k: (k, 0, 0)),
            pl.BlockSpec((1, 32, rows), lambda k: (k, 0, 0)),
            pl.BlockSpec((1, 32, rows), lambda k: (k, 0, 0)),
        ],
        out_shape=[
            jax.ShapeDtypeStruct((count, rows, width), BF16),
            jax.ShapeDtypeStruct((count, 32, rows), BF16),
            jax.ShapeDtypeStruct((count, 32, rows), BF16),
        ],
        scratch_shapes=[
            pltpu.VMEM((2, rows, 256), BF16),
            pltpu.VMEM((8, rows, 256), BF16),
            pltpu.VMEM((2, 4 * rows, 256), BF16),
            pltpu.VMEM((rows, 256), F32),
        ],
        compiler_params=pltpu.CompilerParams(vmem_limit_bytes=48 * 1024 * 1024),
        cost_estimate=pl.CostEstimate(flops=count * 4 * 10**9, bytes_accessed=count * 10**6, transcendentals=count * 2 * 10**6),
    )(x, kbias, mask, gain1, wqkvg, gbias, wo, obias, gain2, wlr_t)


def rearrange_kernel(order_ref, r_ref, out_ref, f_ref):
    for n in range(8):
        first = pl.multiple_of(order_ref[n] * 128, 128)
        r = r_ref[n].reshape(128, 512).astype(F32)
        for c in range(4):
            f_ref[c, pl.ds(first, 128), :] = r[:, c * 128:(c + 1) * 128]
    for b in range(8):
        for c in range(4):
            part = jnp.concatenate(
                [f_ref[c, pl.ds(b * 4 + a, 32, stride=32), :] for a in range(4)], axis=0
            )
            out_ref[c * 128:(c + 1) * 128, b * 128:(b + 1) * 128] = part.T.astype(BF16)


def rearrange(order, right):
    return pl.pallas_call(
        rearrange_kernel,
        in_specs=[pl.BlockSpec(memory_space=pltpu.SMEM), pl.BlockSpec(memory_space=pltpu.VMEM)],
        out_shape=jax.ShapeDtypeStruct((512, 1024), BF16),
        scratch_shapes=[pltpu.VMEM((4, 1024, 128), F32)],
        compiler_params=pltpu.CompilerParams(vmem_limit_bytes=48 * 1024 * 1024),
        cost_estimate=pl.CostEstimate(flops=10**6, bytes_accessed=2 * 10**6, transcendentals=0),
    )(order, right)


def pair_kernel(count, place_ref, *refs):
    parts = refs[:count]
    r_ref, w_ref, inv_ref, bias_ref, old_ref, out_ref, x_ref = refs[count:]
    out_ref[...] = old_ref[...]
    slot = 0
    for part in parts:
        sources, per = part.shape[0], part.shape[1]
        group = 256 // (32 * per)
        for s0 in range(0, sources, group):
            outer = dot(part[s0:s0 + group].reshape(256, 512), r_ref[...]).astype(BF16)
            for n in range(8):
                a = jnp.concatenate(
                    [outer[n * 32:(n + 1) * 32, b * 128:(b + 1) * 128] for b in range(8)], axis=0
                )
                t = a.T
                for q in range(4):
                    x_ref[n * 32:(n + 1) * 32, q * 256:(q + 1) * 256] = t[q * 32:(q + 1) * 32, :]
            y = dot(x_ref[...], w_ref[...])
            rows = 32 * per
            for g in range(group):
                at = place_ref[slot]
                slot += 1
                first = pl.multiple_of(at * per, per)
                part_y = y[g * rows:(g + 1) * rows].reshape(per, 32, 128)
                result = part_y * inv_ref[pl.ds(first, per)] + bias_ref[pl.ds(first, per)]
                out_ref[pl.ds(first, per)] = result.astype(BF16)


def pair(place, parts, r, w, inv, bias, old):
    count = len(parts)
    whole = pl.BlockSpec(memory_space=pltpu.VMEM)
    n = sum(p.shape[0] * p.shape[1] for p in parts)
    return pl.pallas_call(
        functools.partial(pair_kernel, count),
        in_specs=[pl.BlockSpec(memory_space=pltpu.SMEM)] + [whole] * (count + 5),
        out_specs=whole,
        out_shape=jax.ShapeDtypeStruct(old.shape, BF16),
        scratch_shapes=[pltpu.VMEM((256, 1024), BF16)],
        input_output_aliases={count + 5: 0},
        compiler_params=pltpu.CompilerParams(vmem_limit_bytes=48 * 1024 * 1024),
        cost_estimate=pl.CostEstimate(flops=n * 6 * 10**7, bytes_accessed=n * 10**4 * 4, transcendentals=0),
    )(place, *parts, r, w, inv, bias, old)


def body(
    alignment, column_mask, chain_index, attention_norm_gain, query_weight, key_weight, value_matrix,
    gate_matrix, gate_bias, attention_output_weight, attention_output_bias, outer_norm_gain,
    left_factor_weight, right_factor_weight, pair_weight, chain_bias,
):
    row = lax.axis_index("row")
    col = lax.axis_index("col")
    moved = alignment.reshape(16, 32, 4, 256).transpose(1, 2, 0, 3)
    regrouped = lax.all_to_all(moved, "col", split_axis=0, concat_axis=0, tiled=True)

    own_mask = lax.dynamic_slice_in_dim(column_mask, row * 128 + col * 4, 4, 1).T
    kbias = jnp.pad(((own_mask - 1).astype(F32) * 1e9).astype(BF16)[:, :, None], ((0, 0), (0, 0), (0, 127)))
    mask_rows = own_mask.astype(F32).reshape(4, 1, 512)
    row_mask = lax.dynamic_slice_in_dim(column_mask, row * 128, 128, 1).astype(BF16)
    col_mask = lax.dynamic_slice_in_dim(column_mask, col * 32, 32, 1).astype(BF16)
    counts = lax.dot_general(row_mask, col_mask, (((0,), (0,)), ((), ())), preferred_element_type=F32)
    inverse = jnp.broadcast_to((1.0 / (counts + 0.001))[:, :, None], (128, 32, 128))
    row_chain = lax.dynamic_slice_in_dim(chain_index, row * 128, 128, 0)
    col_chain = lax.dynamic_slice_in_dim(chain_index, col * 32, 32, 0)
    same = (row_chain[:, None] == col_chain[None, :]).astype(F32)
    bias = same[:, :, None] * chain_bias
    wqkvg = jnp.concatenate([query_weight, key_weight, value_matrix, gate_matrix], axis=1)
    wlr = jnp.concatenate([left_factor_weight, right_factor_weight], axis=1).T
    wpair = pair_weight.reshape(32, 8, 4, 128).transpose(2, 1, 0, 3).reshape(1024, 128)

    up, left, right = attend(
        regrouped, kbias, mask_rows, attention_norm_gain[None], wqkvg, gate_bias[None],
        attention_output_weight, attention_output_bias[None], outer_norm_gain[None], wlr,
    )
    updated = up.transpose(1, 0, 2)

    moves = []
    for source in range(256):
        zl, co, x, zh, y = np.unravel_index(source, (4, 2, 4, 2, 4))
        moves.append((source, int(np.ravel_multi_index((y, zh, zl, co, x), (4, 2, 4, 2, 4)))))
    r0 = lax.ppermute(right, ("row", "col"), moves)

    def row_flip(value, bit):
        return lax.ppermute(value, "row", [(i, i ^ bit) for i in range(8)])

    def xy(value, axis, shift):
        perm = []
        for c in range(32):
            x, zh, y = c // 8, (c // 4) % 2, c % 4
            if axis == "x":
                x = (x + shift) % 4
            else:
                y = (y + shift) % 4
            perm.append((c, x * 8 + zh * 4 + y))
        return lax.ppermute(value, "col", perm)

    zp = lax.ppermute(left, "col", [(c, c ^ 4) for c in range(32)])
    both = jnp.stack([left, zp])
    h0, h1 = both[:, :2], both[:, 2:]
    b0 = jnp.concatenate([h0] + [xy(h0, "y", s) for s in (1, 2, 3)])
    b1 = jnp.concatenate([h1] + [xy(h1, "x", s) for s in (1, 2, 3)])
    c0 = [xy(b0, "x", s) for s in (1, 3, 2)]
    c1 = [xy(b1, "y", s) for s in (1, 3, 2)]

    ra = row_flip(r0, 2)
    rb = row_flip(jnp.stack([r0, ra]), 4)
    rc = jnp.concatenate([jnp.stack([r0, ra]), rb])
    rd = row_flip(rc, 1)
    gathered = jnp.stack([rc, rd])
    z_lo, core = row // 2, row % 2
    order = jnp.stack([(core ^ (n // 4)) * 4 + (z_lo ^ (n % 4)) for n in range(8)])
    r = rearrange(order.astype(jnp.int32), gathered.reshape(8, 4, 32, 512))

    x, zh, y = col // 8, (col // 4) % 2, col % 4
    shifts = (0, 1, 3, 2)

    def places(half, s):
        result = []
        for t in range(4):
            for z in range(2):
                if half == 0:
                    source = ((x - s) % 4) * 8 + (zh ^ z) * 4 + (y - t) % 4
                else:
                    source = ((x - t) % 4) * 8 + (zh ^ z) * 4 + (y - s) % 4
                result.append(source * 2 + half)
        return result

    out = jnp.zeros((128, 32, 128), BF16)
    for n, s in enumerate(shifts):
        p0, p1 = (b0, b1) if n == 0 else (c0[n - 1], c1[n - 1])
        place = jnp.stack(places(0, s) + places(1, s)).astype(jnp.int32)
        out = pair(place, [p0, p1], r, wpair, inverse, bias, out)
    return updated, out


def solution(mesh):
    return jax.shard_map(
        body,
        mesh=mesh,
        in_specs=(P("col", "row", None),) + (P(),) * 15,
        out_specs=(P(None, ("row", "col"), None), P("row", "col", None)),
        check_vma=False,
    )
```

```python
import functools
import math

import jax
import jax.numpy as jnp
import numpy as np
from jax import lax
from jax.experimental import pallas as pl
from jax.experimental.pallas import tpu as pltpu
from jax.sharding import PartitionSpec as P

HEAD_FEATURES = 32
F32, BF16 = jnp.float32, jnp.bfloat16
SB = 256
VMEM_LIMIT = 40 * 1024 * 1024

def norm_rows(x, gain):
    average = jnp.mean(x, -1, keepdims=True)
    centred = x - average
    variance = jnp.mean(centred * centred, -1, keepdims=True)
    return centred * lax.rsqrt(variance + 1e-05) * gain

def dot(a, b):
    return jnp.dot(a, b, preferred_element_type=F32)

def dot_nt(a, b):
    return lax.dot_general(a, b, (((1,), (1,)), ((), ())), preferred_element_type=F32)

def attend_kernel(
    parts_ref, mask_ref, gain1_ref, wqkvg_ref, gbias_ref, wo_ref, obias_ref, gain2_ref, wlr_ref,
    up_ref, left_ref, right_ref, qa_ref, ka_ref, va_ref, gated_ref,
):
    rows = qa_ref.shape[1]
    lane = lax.broadcasted_iota(jnp.int32, (1, 128), 1)

    @pl.when(pl.program_id(0) == 0)
    def _():
        ka_ref[...] = jnp.zeros_like(ka_ref)
        va_ref[...] = jnp.zeros_like(va_ref)
        ones = jnp.broadcast_to(jnp.where(lane == 0, 1.0, 0.0).astype(BF16), (rows, 128))
        for g in range(2):
            qa_ref[g, :, 128:] = ones
            for h in range(4):
                va_ref[g, h * rows:(h + 1) * rows, 128:] = jnp.broadcast_to(
                    jnp.where(lane // 32 == h, 1.0, 0.0).astype(BF16), (rows, 128))

    x = parts_ref[...].reshape(rows, 256).astype(F32)
    normed = norm_rows(x, gain1_ref[...]).astype(BF16)
    scale = math.log2(math.e) * HEAD_FEATURES ** (-0.5)
    queries = (dot(normed, wqkvg_ref[:, 0:256]) * scale).astype(BF16)
    keys = dot(normed, wqkvg_ref[:, 256:512]).astype(BF16).T
    values = dot(normed, wqkvg_ref[:, 512:768]).astype(BF16)
    live = mask_ref[...].reshape(1, rows)
    dead = jnp.where(lax.broadcasted_iota(jnp.int32, (16, 1), 0) == 0, (live - 1.0) * 1e9, 0.0).astype(BF16)
    for g in range(2):
        qa_ref[g, :, :128] = queries[:, g * 128:(g + 1) * 128]
        for h in range(4):
            n = g * 4 + h
            ka_ref[n, h * 32:(h + 1) * 32, :] = keys[n * 32:(n + 1) * 32, :]
            ka_ref[n, 128:144, :] = dead
            kept = jnp.where(lane // 32 == h, 1.0, 0.0).astype(BF16)
            va_ref[g, h * rows:(h + 1) * rows, :128] = values[:, g * 128:(g + 1) * 128] * kept
    gated_ref[...] = jax.nn.sigmoid(dot(normed, wqkvg_ref[:, 768:1024]) + gbias_ref[...])
    for g in range(2):
        for b in range(rows // SB):
            q = qa_ref[g, b * SB:(b + 1) * SB, :]
            total = None
            for h in range(4):
                s = dot(q, ka_ref[g * 4 + h])
                m = jnp.max(s, axis=-1, keepdims=True)
                p = jnp.exp2(s - m).astype(BF16)
                part = dot(p, va_ref[g, h * rows:(h + 1) * rows, :])
                total = part if total is None else total + part
            out = total[:, :128] / total[:, 128:]
            sl = (slice(b * SB, (b + 1) * SB), slice(g * 128, (g + 1) * 128))
            gated_ref[sl] = gated_ref[sl] * out
    gated = gated_ref[...].astype(BF16)
    updated = (dot(gated, wo_ref[...]) + obias_ref[...] + x).astype(BF16)
    up_ref[...] = updated.reshape(up_ref.shape)
    again = norm_rows(updated.astype(F32), gain2_ref[...]).astype(BF16)
    factors = dot_nt(wlr_ref[...], again) * live
    left_ref[...] = factors[:32].astype(BF16).reshape(left_ref.shape)
    right_ref[...] = factors[32:].astype(BF16).reshape(right_ref.shape)

def attend(x, mask, gain1, wqkvg, gbias, wo, obias, gain2, wlr_t, first=0, count=4):
    groups, _, per, width = x.shape
    rows = groups * per
    whole = lambda a: pl.BlockSpec(a.shape, lambda k: (0,) * a.ndim)
    return pl.pallas_call(
        attend_kernel,
        grid=(count,),
        in_specs=[
            pl.BlockSpec((groups, 1, per, width), lambda k: (0, k + first, 0, 0)),
            pl.BlockSpec((1, 1, rows), lambda k: (k + first, 0, 0)),
            whole(gain1), whole(wqkvg), whole(gbias), whole(wo), whole(obias), whole(gain2), whole(wlr_t),
        ],
        out_specs=[
            pl.BlockSpec((1, rows, width), lambda k: (k, 0, 0)),
            pl.BlockSpec((1, 32, rows), lambda k: (k, 0, 0)),
            pl.BlockSpec((1, 32, rows), lambda k: (k, 0, 0)),
        ],
        out_shape=[
            jax.ShapeDtypeStruct((count, rows, width), BF16),
            jax.ShapeDtypeStruct((count, 32, rows), BF16),
            jax.ShapeDtypeStruct((count, 32, rows), BF16),
        ],
        scratch_shapes=[
            pltpu.VMEM((2, rows, 256), BF16),
            pltpu.VMEM((8, 256, rows), BF16),
            pltpu.VMEM((2, 4 * rows, 256), BF16),
            pltpu.VMEM((rows, 256), F32),
        ],
        compiler_params=pltpu.CompilerParams(vmem_limit_bytes=VMEM_LIMIT),
        cost_estimate=pl.CostEstimate(
            flops=count * 4 * 10**9, bytes_accessed=count * 10**6, transcendentals=count * 2 * 10**6
        ),
    )(x, mask, gain1, wqkvg, gbias, wo, obias, gain2, wlr_t)


def rearrange_kernel(order_ref, a_ref, b_ref, c_ref, out_ref, f_ref):
    pieces = [a_ref.at[0], a_ref.at[1], b_ref.at[0], b_ref.at[1]]
    pieces += [c_ref.at[n] for n in range(4)]
    for n in range(8):
        first = pl.multiple_of(order_ref[n] * 128, 128)
        r = pieces[n][...].reshape(128, 512).astype(F32)
        for c in range(4):
            f_ref[c, pl.ds(first, 128), :] = r[:, c * 128:(c + 1) * 128]
    for b in range(8):
        for c in range(4):
            part = jnp.concatenate(
                [f_ref[c, pl.ds(b * 4 + a, 32, stride=32), :] for a in range(4)], axis=0
            )
            out_ref[c * 128:(c + 1) * 128, b * 128:(b + 1) * 128] = part.T.astype(BF16)


def rearrange(order, a, b, c):
    return pl.pallas_call(
        rearrange_kernel,
        in_specs=[pl.BlockSpec(memory_space=pltpu.SMEM)] + [pl.BlockSpec(memory_space=pltpu.VMEM)] * 3,
        out_shape=jax.ShapeDtypeStruct((512, 1024), BF16),
        scratch_shapes=[pltpu.VMEM((4, 1024, 128), F32)],
        compiler_params=pltpu.CompilerParams(vmem_limit_bytes=VMEM_LIMIT),
        cost_estimate=pl.CostEstimate(flops=10**6, bytes_accessed=4 * 10**6, transcendentals=0),
    )(order, a, b, c)


def pair_kernel(first, count, has_old, place_ref, *refs):
    parts = refs[:count]
    r_ref, w_ref, inv_ref, same_ref, bias_ref = refs[count:count + 5]
    out_ref, x_ref, y_ref, sems = refs[count + 5 + has_old:]
    copies = []
    at = 0
    for part in parts:
        for half in range(part.shape[0] // 4):
            outer = dot(part[half * 4:half * 4 + 4].reshape(512, 512), r_ref[...]).astype(BF16)
            for n in range(16):
                a = jnp.concatenate(
                    [outer[n * 32:(n + 1) * 32, b * 128:(b + 1) * 128] for b in range(8)], axis=0
                )
                t = a.T
                for q in range(4):
                    x_ref[n * 32:(n + 1) * 32, q * 256:(q + 1) * 256] = t[q * 32:(q + 1) * 32, :]
            y = dot(x_ref[...], w_ref[...])
            for n in range(16):
                lane = (first + at) * 4 + n
                scale = jnp.broadcast_to(inv_ref[:, lane:lane + 1], (32, 128))
                same = jnp.broadcast_to(same_ref[:, lane:lane + 1], (32, 128))
                result = y[n * 32:(n + 1) * 32] * scale + same * bias_ref[...]
                y_ref[at + n // 4, n % 4] = result.astype(BF16)
            for s in range(at, at + 4):
                copy = pltpu.make_async_copy(y_ref.at[s], out_ref.at[place_ref[first + s]], sems.at[s])
                copy.start()
                copies.append(copy)
            at += 4
    for copy in copies:
        copy.wait()


def pair(first, place, parts, r, w, inv, same, bias, old=None):
    count = len(parts)
    sources = sum(part.shape[0] for part in parts)
    vmem = pl.BlockSpec(memory_space=pltpu.VMEM)
    anywhere = pl.BlockSpec(memory_space=pl.ANY)
    has_old = old is not None
    return pl.pallas_call(
        functools.partial(pair_kernel, first, count, has_old),
        in_specs=[pl.BlockSpec(memory_space=pltpu.SMEM)] + [vmem] * (count + 5) + [anywhere] * has_old,
        out_specs=anywhere,
        out_shape=jax.ShapeDtypeStruct((32, 4, 32, 128), BF16),
        scratch_shapes=[
            pltpu.VMEM((512, 1024), BF16),
            pltpu.VMEM((sources, 4, 32, 128), BF16),
            pltpu.SemaphoreType.DMA((sources,)),
        ],
        input_output_aliases={count + 6: 0} if has_old else {},
        compiler_params=pltpu.CompilerParams(vmem_limit_bytes=VMEM_LIMIT),
        cost_estimate=pl.CostEstimate(
            flops=sources * 25 * 10**7, bytes_accessed=sources * 4 * 10**5, transcendentals=0
        ),
    )(place, *parts, r, w, inv, same, bias, *([old] if has_old else []))


def coordinates(device):
    return [int(n) for n in np.unravel_index(device, (4, 2, 4, 2, 4))]


def permute_all(value, move):
    pairs = []
    for source in range(256):
        pairs.append((source, int(np.ravel_multi_index(move(*coordinates(source)), (4, 2, 4, 2, 4)))))
    return lax.ppermute(value, ("row", "col"), pairs)


def shifted(phase, shift):
    def move(zl, co, x, zh, y):
        if (co + phase) % 2 == 0:
            return zl, co, x, zh, (y + shift) % 4
        return zl, co, (x + shift) % 4, zh, y

    return move


SHIFTS = (0, 1, 3, 2)


def after(value, *others):
    anywhere = pl.BlockSpec(memory_space=pl.ANY)

    def nothing(*refs):
        pass

    return pl.pallas_call(
        nothing,
        in_specs=[anywhere] * (1 + len(others)),
        out_specs=anywhere,
        out_shape=jax.ShapeDtypeStruct(value.shape, value.dtype),
        input_output_aliases={0: 0},
        cost_estimate=pl.CostEstimate(flops=0, bytes_accessed=0, transcendentals=0),
    )(value, *others)


def body(
    alignment, column_mask, chain_index, attention_norm_gain, query_weight, key_weight, value_matrix,
    gate_matrix, gate_bias, attention_output_weight, attention_output_bias, outer_norm_gain,
    left_factor_weight, right_factor_weight, pair_weight, chain_bias,
):
    row = lax.axis_index("row")
    col = lax.axis_index("col")
    z_lo, core = row // 2, row % 2
    x, z_hi, y = col // 8, (col // 4) % 2, col % 4
    moved = alignment.reshape(16, 32, 4, 256).transpose(1, 2, 0, 3)
    regrouped = lax.all_to_all(moved, "col", split_axis=0, concat_axis=0, tiled=True)

    place = []
    for s in SHIFTS:
        for t in SHIFTS:
            for z in range(2):
                by_y = ((x - s) % 4) * 8 + (z_hi ^ z) * 4 + (y - t) % 4
                by_x = ((x - t) % 4) * 8 + (z_hi ^ z) * 4 + (y - s) % 4
                place.append(jnp.where(core == 0, by_y, by_x))
    place = jnp.stack(place).astype(jnp.int32)
    order = jnp.stack(
        [(core ^ c) * 4 + (z_lo ^ n) for c in range(2) for n in (0, 2, 1, 3)]
    ).astype(jnp.int32)

    own_mask = lax.dynamic_slice_in_dim(column_mask, row * 128 + col * 4, 4, 1).T
    live = own_mask.astype(F32).reshape(4, 1, 512)
    row_mask = lax.dynamic_slice_in_dim(column_mask, row * 128, 128, 1).astype(BF16)
    col_mask = lax.dynamic_slice_in_dim(column_mask, col * 32, 32, 1).astype(BF16)
    counts = lax.dot_general(col_mask, row_mask, (((0,), (0,)), ((), ())), preferred_element_type=F32)
    row_chain = lax.dynamic_slice_in_dim(chain_index, row * 128, 128, 0)
    col_chain = lax.dynamic_slice_in_dim(chain_index, col * 32, 32, 0)
    same = (col_chain[:, None] == row_chain[None, :]).astype(F32)
    residue = (place[:, None] * 4 + jnp.arange(4)[None, :]).reshape(128)
    chosen = (jnp.arange(128)[:, None] == residue[None, :]).astype(F32)
    arrived = jnp.dot(jnp.concatenate([1.0 / (counts + 0.001), same]), chosen, precision=lax.Precision.HIGHEST)
    inverse, same = arrived[:32], arrived[32:]
    wqkvg = jnp.concatenate([query_weight, key_weight, value_matrix, gate_matrix], axis=1)
    wlr = jnp.concatenate([left_factor_weight, right_factor_weight], axis=1).T
    wpair = pair_weight.reshape(32, 8, 4, 128).transpose(2, 1, 0, 3).reshape(1024, 128)
    prepared = (live, wqkvg, wlr, wpair, inverse, same, place, order)
    regrouped, prepared = lax.optimization_barrier((regrouped, prepared))
    live, wqkvg, wlr, wpair, inverse, same, place, order = prepared

    up, left, right = attend(
        regrouped, live, attention_norm_gain[None], wqkvg, gate_bias[None],
        attention_output_weight, attention_output_bias[None], outer_norm_gain[None], wlr,
    )
    updated = up.transpose(1, 0, 2)

    beside = permute_all(left, lambda zl, co, x, zh, y: (zl, co, x, 1 - zh, y))
    near = permute_all(right, lambda zl, co, x, zh, y: (y, zh, zl, co, x))
    far = permute_all(after(right, beside), lambda zl, co, x, zh, y: (y ^ 2, zh, zl, co, x))
    own = jnp.stack([left, beside])
    line = jnp.concatenate([own] + [permute_all(own, shifted(0, s)) for s in SHIFTS[1:]])
    right_a = jnp.stack([near, far])
    right_b = permute_all(right_a, lambda zl, co, x, zh, y: (zl ^ 1, co, x, zh, y))
    below, above = permute_all(line, shifted(1, 1)), permute_all(line, shifted(1, 3))
    parts = [line, below, above, permute_all(below[:4], shifted(1, 1)), permute_all(above[4:], shifted(1, 3))]
    right_c = permute_all(
        jnp.concatenate([right_a, right_b]), lambda zl, co, x, zh, y: (zl, 1 - co, x, zh, y)
    )
    r = rearrange(order, right_a, right_b, right_c)
    out = None
    for first, some in ((0, parts[:1]), (8, parts[1:3]), (24, parts[3:])):
        out = pair(first, place, some, r, wpair, inverse, same, chain_bias[None], out)
    return updated, out.reshape(128, 32, 128)


def solution(mesh):
    return jax.shard_map(
        body,
        mesh=mesh,
        in_specs=(P("col", "row", None),) + (P(),) * 15,
        out_specs=(P(None, ("row", "col"), None), P("row", "col", None)),
        check_vma=False,
    )
```

```python
import functools
import math

import jax
import jax.numpy as jnp
import numpy as np
from jax import lax
from jax.experimental import pallas as pl
from jax.experimental.pallas import tpu as pltpu
from jax.sharding import PartitionSpec as P

HEAD_FEATURES = 32
F32, BF16 = jnp.float32, jnp.bfloat16
SB = 256
VMEM_LIMIT = 40 * 1024 * 1024

def norm_rows(x, gain):
    average = jnp.mean(x, -1, keepdims=True)
    centred = x - average
    variance = jnp.mean(centred * centred, -1, keepdims=True)
    return centred * lax.rsqrt(variance + 1e-05) * gain

def dot(a, b):
    return jnp.dot(a, b, preferred_element_type=F32)

def dot_nt(a, b):
    return lax.dot_general(a, b, (((1,), (1,)), ((), ())), preferred_element_type=F32)

def attend_kernel(
    parts_ref, mask_ref, gain1_ref, wqkvg_ref, gbias_ref, wo_ref, obias_ref, gain2_ref, wlr_ref,
    up_ref, left_ref, right_ref, qa_ref, ka_ref, va_ref, gated_ref,
):
    rows = qa_ref.shape[1]
    lane = lax.broadcasted_iota(jnp.int32, (1, 128), 1)

    @pl.when(pl.program_id(0) == 0)
    def _():
        ka_ref[...] = jnp.zeros_like(ka_ref)
        va_ref[...] = jnp.zeros_like(va_ref)
        ones = jnp.broadcast_to(jnp.where(lane == 0, 1.0, 0.0).astype(BF16), (rows, 128))
        for g in range(2):
            qa_ref[g, :, 128:] = ones
            for h in range(4):
                va_ref[g, h * rows:(h + 1) * rows, 128:] = jnp.broadcast_to(
                    jnp.where(lane // 32 == h, 1.0, 0.0).astype(BF16), (rows, 128))

    x = parts_ref[...].reshape(rows, 256).astype(F32)
    normed = norm_rows(x, gain1_ref[...]).astype(BF16)
    scale = math.log2(math.e) * HEAD_FEATURES ** (-0.5)
    queries = (dot(normed, wqkvg_ref[:, 0:256]) * scale).astype(BF16)
    keys = dot(normed, wqkvg_ref[:, 256:512]).astype(BF16).T
    values = dot(normed, wqkvg_ref[:, 512:768]).astype(BF16)
    live = mask_ref[...].reshape(1, rows)
    dead = jnp.where(lax.broadcasted_iota(jnp.int32, (16, 1), 0) == 0, (live - 1.0) * 1e9, 0.0).astype(BF16)
    for g in range(2):
        qa_ref[g, :, :128] = queries[:, g * 128:(g + 1) * 128]
        for h in range(4):
            n = g * 4 + h
            ka_ref[n, h * 32:(h + 1) * 32, :] = keys[n * 32:(n + 1) * 32, :]
            ka_ref[n, 128:144, :] = dead
            kept = jnp.where(lane // 32 == h, 1.0, 0.0).astype(BF16)
            va_ref[g, h * rows:(h + 1) * rows, :128] = values[:, g * 128:(g + 1) * 128] * kept
    gated_ref[...] = jax.nn.sigmoid(dot(normed, wqkvg_ref[:, 768:1024]) + gbias_ref[...])
    for g in range(2):
        for b in range(rows // SB):
            q = qa_ref[g, b * SB:(b + 1) * SB, :]
            total = None
            for h in range(4):
                s = dot(q, ka_ref[g * 4 + h])
                m = jnp.max(s, axis=-1, keepdims=True)
                p = jnp.exp2(s - m).astype(BF16)
                part = dot(p, va_ref[g, h * rows:(h + 1) * rows, :])
                total = part if total is None else total + part
            out = total[:, :128] / total[:, 128:]
            sl = (slice(b * SB, (b + 1) * SB), slice(g * 128, (g + 1) * 128))
            gated_ref[sl] = gated_ref[sl] * out
    gated = gated_ref[...].astype(BF16)
    updated = (dot(gated, wo_ref[...]) + obias_ref[...] + x).astype(BF16)
    up_ref[...] = updated.reshape(up_ref.shape)
    again = norm_rows(updated.astype(F32), gain2_ref[...]).astype(BF16)
    factors = dot_nt(wlr_ref[...], again) * live
    left_ref[...] = factors[:32].astype(BF16).reshape(left_ref.shape)
    right_ref[...] = factors[32:].astype(BF16).reshape(right_ref.shape)

def attend(x, mask, gain1, wqkvg, gbias, wo, obias, gain2, wlr_t, first=0, count=4):
    groups, _, per, width = x.shape
    rows = groups * per
    whole = lambda a: pl.BlockSpec(a.shape, lambda k: (0,) * a.ndim)
    return pl.pallas_call(
        attend_kernel,
        grid=(count,),
        in_specs=[
            pl.BlockSpec((groups, 1, per, width), lambda k: (0, k + first, 0, 0)),
            pl.BlockSpec((1, 1, rows), lambda k: (k + first, 0, 0)),
            whole(gain1), whole(wqkvg), whole(gbias), whole(wo), whole(obias), whole(gain2), whole(wlr_t),
        ],
        out_specs=[
            pl.BlockSpec((1, rows, width), lambda k: (k, 0, 0)),
            pl.BlockSpec((1, 32, rows), lambda k: (k, 0, 0)),
            pl.BlockSpec((1, 32, rows), lambda k: (k, 0, 0)),
        ],
        out_shape=[
            jax.ShapeDtypeStruct((count, rows, width), BF16),
            jax.ShapeDtypeStruct((count, 32, rows), BF16),
            jax.ShapeDtypeStruct((count, 32, rows), BF16),
        ],
        scratch_shapes=[
            pltpu.VMEM((2, rows, 256), BF16),
            pltpu.VMEM((8, 256, rows), BF16),
            pltpu.VMEM((2, 4 * rows, 256), BF16),
            pltpu.VMEM((rows, 256), F32),
        ],
        compiler_params=pltpu.CompilerParams(vmem_limit_bytes=VMEM_LIMIT),
        cost_estimate=pl.CostEstimate(
            flops=count * 4 * 10**9, bytes_accessed=count * 10**6, transcendentals=count * 2 * 10**6
        ),
    )(x, mask, gain1, wqkvg, gbias, wo, obias, gain2, wlr_t)


def rearrange_kernel(order_ref, a_ref, b_ref, c_ref, out_ref, f_ref):
    pieces = [a_ref.at[0], a_ref.at[1], b_ref.at[0], b_ref.at[1]]
    pieces += [c_ref.at[n] for n in range(4)]
    for n in range(8):
        first = pl.multiple_of(order_ref[n] * 128, 128)
        r = pieces[n][...].reshape(128, 512).astype(F32)
        for c in range(4):
            f_ref[c, pl.ds(first, 128), :] = r[:, c * 128:(c + 1) * 128]
    for b in range(8):
        for c in range(4):
            part = jnp.concatenate(
                [f_ref[c, pl.ds(b * 4 + a, 32, stride=32), :] for a in range(4)], axis=0
            )
            out_ref[c * 128:(c + 1) * 128, b * 128:(b + 1) * 128] = part.astype(BF16).T


def rearrange(order, a, b, c):
    return pl.pallas_call(
        rearrange_kernel,
        in_specs=[pl.BlockSpec(memory_space=pltpu.SMEM)] + [pl.BlockSpec(memory_space=pltpu.VMEM)] * 3,
        out_shape=jax.ShapeDtypeStruct((512, 1024), BF16),
        scratch_shapes=[pltpu.VMEM((4, 1024, 128), F32)],
        compiler_params=pltpu.CompilerParams(vmem_limit_bytes=VMEM_LIMIT),
        cost_estimate=pl.CostEstimate(flops=10**6, bytes_accessed=4 * 10**6, transcendentals=0),
    )(order, a, b, c)


def pair_kernel(first, count, has_old, place_ref, *refs):
    parts = refs[:count]
    r_ref, w_ref, inv_ref, same_ref, bias_ref = refs[count:count + 5]
    out_ref, x_ref, y_ref, sems = refs[count + 5 + has_old:]
    copies = []
    halves = [(part, n) for part in parts for n in range(0, part.shape[0], 2)]

    def outer_product(part, n):
        return dot(part[n:n + 2].reshape(256, 512), r_ref[...]).astype(BF16)

    def project(at):
        y = dot(x_ref[(at // 2) % 2], w_ref[...])
        for n in range(8):
            lane = (first + at) * 4 + n
            scale = jnp.broadcast_to(inv_ref[:, lane:lane + 1], (32, 128))
            same = jnp.broadcast_to(same_ref[:, lane:lane + 1], (32, 128))
            result = y[n * 32:(n + 1) * 32] * scale + same * bias_ref[...]
            y_ref[at + n // 4, n % 4] = result.astype(BF16)
        for s in range(at, at + 2):
            copy = pltpu.make_async_copy(y_ref.at[s], out_ref.at[place_ref[first + s]], sems.at[s])
            copy.start()
            copies.append(copy)

    following = outer_product(*halves[0])
    for i in range(len(halves)):
        outer = following
        if i + 1 < len(halves):
            following = outer_product(*halves[i + 1])
        for n in range(8):
            a = jnp.concatenate(
                [outer[n * 32:(n + 1) * 32, b * 128:(b + 1) * 128] for b in range(8)], axis=0
            )
            t = a.T
            for q in range(4):
                x_ref[i % 2, n * 32:(n + 1) * 32, q * 256:(q + 1) * 256] = t[q * 32:(q + 1) * 32, :]
        if i:
            project(2 * i - 2)
    project(2 * len(halves) - 2)
    for copy in copies:
        copy.wait()


def pair(first, place, parts, r, w, inv, same, bias, old=None):
    count = len(parts)
    sources = sum(part.shape[0] for part in parts)
    vmem = pl.BlockSpec(memory_space=pltpu.VMEM)
    anywhere = pl.BlockSpec(memory_space=pl.ANY)
    has_old = old is not None
    return pl.pallas_call(
        functools.partial(pair_kernel, first, count, has_old),
        in_specs=[pl.BlockSpec(memory_space=pltpu.SMEM)] + [vmem] * (count + 5) + [anywhere] * has_old,
        out_specs=anywhere,
        out_shape=jax.ShapeDtypeStruct((32, 4, 32, 128), BF16),
        scratch_shapes=[
            pltpu.VMEM((2, 256, 1024), BF16),
            pltpu.VMEM((sources, 4, 32, 128), BF16),
            pltpu.SemaphoreType.DMA((sources,)),
        ],
        input_output_aliases={count + 6: 0} if has_old else {},
        compiler_params=pltpu.CompilerParams(vmem_limit_bytes=VMEM_LIMIT),
        cost_estimate=pl.CostEstimate(
            flops=sources * 25 * 10**7, bytes_accessed=sources * 4 * 10**5, transcendentals=0
        ),
    )(place, *parts, r, w, inv, same, bias, *([old] if has_old else []))


def coordinates(device):
    return [int(n) for n in np.unravel_index(device, (4, 2, 4, 2, 4))]


def permute_all(value, move):
    pairs = []
    for source in range(256):
        pairs.append((source, int(np.ravel_multi_index(move(*coordinates(source)), (4, 2, 4, 2, 4)))))
    return lax.ppermute(value, ("row", "col"), pairs)


def shifted(phase, shift):
    def move(zl, co, x, zh, y):
        if (co + phase) % 2 == 0:
            return zl, co, x, zh, (y + shift) % 4
        return zl, co, (x + shift) % 4, zh, y

    return move


SHIFTS = (0, 1, 3, 2)


def after(value, *others):
    anywhere = pl.BlockSpec(memory_space=pl.ANY)

    def nothing(*refs):
        pass

    return pl.pallas_call(
        nothing,
        in_specs=[anywhere] * (1 + len(others)),
        out_specs=anywhere,
        out_shape=jax.ShapeDtypeStruct(value.shape, value.dtype),
        input_output_aliases={0: 0},
        cost_estimate=pl.CostEstimate(flops=0, bytes_accessed=0, transcendentals=0),
    )(value, *others)


def body(
    alignment, column_mask, chain_index, attention_norm_gain, query_weight, key_weight, value_matrix,
    gate_matrix, gate_bias, attention_output_weight, attention_output_bias, outer_norm_gain,
    left_factor_weight, right_factor_weight, pair_weight, chain_bias,
):
    row = lax.axis_index("row")
    col = lax.axis_index("col")
    z_lo, core = row // 2, row % 2
    x, z_hi, y = col // 8, (col // 4) % 2, col % 4
    moved = alignment.reshape(16, 32, 4, 256).transpose(1, 2, 0, 3)
    regrouped = lax.all_to_all(moved, "col", split_axis=0, concat_axis=0, tiled=True)

    place = []
    for s in SHIFTS:
        for t in SHIFTS:
            for z in range(2):
                by_y = ((x - s) % 4) * 8 + (z_hi ^ z) * 4 + (y - t) % 4
                by_x = ((x - t) % 4) * 8 + (z_hi ^ z) * 4 + (y - s) % 4
                place.append(jnp.where(core == 0, by_y, by_x))
    place = jnp.stack(place).astype(jnp.int32)
    order = jnp.stack(
        [(core ^ c) * 4 + (z_lo ^ n) for c in range(2) for n in (0, 2, 1, 3)]
    ).astype(jnp.int32)

    own_mask = lax.dynamic_slice_in_dim(column_mask, row * 128 + col * 4, 4, 1).T
    live = own_mask.astype(F32).reshape(4, 1, 512)
    row_mask = lax.dynamic_slice_in_dim(column_mask, row * 128, 128, 1).astype(BF16)
    col_mask = lax.dynamic_slice_in_dim(column_mask, col * 32, 32, 1).astype(BF16)
    counts = lax.dot_general(col_mask, row_mask, (((0,), (0,)), ((), ())), preferred_element_type=F32)
    row_chain = lax.dynamic_slice_in_dim(chain_index, row * 128, 128, 0)
    col_chain = lax.dynamic_slice_in_dim(chain_index, col * 32, 32, 0)
    same = (col_chain[:, None] == row_chain[None, :]).astype(F32)
    residue = (place[:, None] * 4 + jnp.arange(4)[None, :]).reshape(128)
    chosen = (jnp.arange(128)[:, None] == residue[None, :]).astype(F32)
    arrived = jnp.dot(jnp.concatenate([1.0 / (counts + 0.001), same]), chosen, precision=lax.Precision.HIGHEST)
    inverse, same = arrived[:32], arrived[32:]
    wqkvg = jnp.concatenate([query_weight, key_weight, value_matrix, gate_matrix], axis=1)
    wlr = jnp.concatenate([left_factor_weight, right_factor_weight], axis=1).T
    wpair = pair_weight.reshape(32, 8, 4, 128).transpose(2, 1, 0, 3).reshape(1024, 128)
    prepared = (live, wqkvg, wlr, wpair, inverse, same, place, order)
    regrouped, prepared = lax.optimization_barrier((regrouped, prepared))
    live, wqkvg, wlr, wpair, inverse, same, place, order = prepared

    up, left, right = attend(
        regrouped, live, attention_norm_gain[None], wqkvg, gate_bias[None],
        attention_output_weight, attention_output_bias[None], outer_norm_gain[None], wlr,
    )
    updated = up.transpose(1, 0, 2)

    beside = permute_all(left, lambda zl, co, x, zh, y: (zl, co, x, 1 - zh, y))
    near = permute_all(right, lambda zl, co, x, zh, y: (y, zh, zl, co, x))
    far = permute_all(after(right, beside), lambda zl, co, x, zh, y: (y ^ 2, zh, zl, co, x))
    own = jnp.stack([left, beside])
    line = jnp.concatenate([own] + [permute_all(own, shifted(0, s)) for s in SHIFTS[1:]])
    right_a = jnp.stack([near, far])
    right_b = permute_all(right_a, lambda zl, co, x, zh, y: (zl ^ 1, co, x, zh, y))
    below, above = permute_all(line, shifted(1, 1)), permute_all(line, shifted(1, 3))
    parts = [line, below, above, permute_all(below[:4], shifted(1, 1)), permute_all(above[4:], shifted(1, 3))]
    right_c = permute_all(
        after(jnp.concatenate([right_a, right_b]), updated), lambda zl, co, x, zh, y: (zl, 1 - co, x, zh, y)
    )
    r = rearrange(order, right_a, right_b, right_c)
    out = None
    for first, some in ((0, parts[:3]), (24, parts[3:])):
        out = pair(first, place, some, r, wpair, inverse, same, chain_bias[None], out)
    return updated, out.reshape(128, 32, 128)


def solution(mesh):
    return jax.shard_map(
        body,
        mesh=mesh,
        in_specs=(P("col", "row", None),) + (P(),) * 15,
        out_specs=(P(None, ("row", "col"), None), P("row", "col", None)),
        check_vma=False,
    )
```

```python
import functools
import math

import jax
import jax.numpy as jnp
import numpy as np
from jax import lax
from jax.experimental import pallas as pl
from jax.experimental.pallas import tpu as pltpu
from jax.sharding import PartitionSpec as P

HEAD_FEATURES = 32
F32, BF16 = jnp.float32, jnp.bfloat16
SB = 256
VMEM_LIMIT = 40 * 1024 * 1024

def norm_rows(x, gain):
    average = jnp.mean(x, -1, keepdims=True)
    centred = x - average
    variance = jnp.mean(centred * centred, -1, keepdims=True)
    return centred * lax.rsqrt(variance + 1e-05) * gain

def dot(a, b):
    return jnp.dot(a, b, preferred_element_type=F32)

def dot_nt(a, b):
    return lax.dot_general(a, b, (((1,), (1,)), ((), ())), preferred_element_type=F32)

def attend_kernel(
    parts_ref, mask_ref, gain1_ref, wqkvg_ref, gbias_ref, wo_ref, obias_ref, gain2_ref, wlr_ref,
    up_ref, left_ref, right_ref, qa_ref, ka_ref, va_ref, gated_ref,
):
    rows = qa_ref.shape[1]
    lane = lax.broadcasted_iota(jnp.int32, (1, 128), 1)

    @pl.when(pl.program_id(0) == 0)
    def _():
        ka_ref[...] = jnp.zeros_like(ka_ref)
        ones = jnp.broadcast_to(jnp.where(lane == 0, 1.0, 0.0).astype(BF16), (rows, 128))
        for g in range(2):
            qa_ref[g, :, 128:] = ones
            for h in range(4):
                va_ref[g, h * rows:(h + 1) * rows, 128:] = jnp.broadcast_to(
                    jnp.where(lane // 32 == h, 1.0, 0.0).astype(BF16), (rows, 128))

    x = parts_ref[...].reshape(rows, 256).astype(F32)
    normed = norm_rows(x, gain1_ref[...]).astype(BF16)
    scale = math.log2(math.e) * HEAD_FEATURES ** (-0.5)
    queries = (dot(normed, wqkvg_ref[:, 0:256]) * scale).astype(BF16)
    keys = dot(normed, wqkvg_ref[:, 256:512]).astype(BF16).T
    values = dot(normed, wqkvg_ref[:, 512:768]).astype(BF16)
    live = mask_ref[...].reshape(1, rows)
    dead = jnp.where(lax.broadcasted_iota(jnp.int32, (16, 1), 0) == 0, (live - 1.0) * 1e9, 0.0).astype(BF16)
    for g in range(2):
        qa_ref[g, :, :128] = queries[:, g * 128:(g + 1) * 128]
        for h in range(4):
            n = g * 4 + h
            ka_ref[n, h * 32:(h + 1) * 32, :] = keys[n * 32:(n + 1) * 32, :]
            ka_ref[n, 128:144, :] = dead
            kept = jnp.where(lane // 32 == h, 1.0, 0.0).astype(BF16)
            va_ref[g, h * rows:(h + 1) * rows, :128] = values[:, g * 128:(g + 1) * 128] * kept
    gated_ref[...] = jax.nn.sigmoid(dot(normed, wqkvg_ref[:, 768:1024]) + gbias_ref[...])
    for g in range(2):
        for b in range(rows // SB):
            q = qa_ref[g, b * SB:(b + 1) * SB, :]
            total = None
            for h in range(4):
                s = dot(q, ka_ref[g * 4 + h])
                m = jnp.max(s, axis=-1, keepdims=True)
                p = jnp.exp2(s - m).astype(BF16)
                part = dot(p, va_ref[g, h * rows:(h + 1) * rows, :])
                total = part if total is None else total + part
            out = total[:, :128] / total[:, 128:]
            sl = (slice(b * SB, (b + 1) * SB), slice(g * 128, (g + 1) * 128))
            gated_ref[sl] = gated_ref[sl] * out
    gated = gated_ref[...].astype(BF16)
    updated = (dot(gated, wo_ref[...]) + obias_ref[...] + x).astype(BF16)
    up_ref[...] = updated.reshape(up_ref.shape)
    again = norm_rows(updated.astype(F32), gain2_ref[...]).astype(BF16)
    factors = dot_nt(wlr_ref[...], again) * live
    left_ref[...] = factors[:32].astype(BF16).reshape(left_ref.shape)
    right_ref[...] = factors[32:].astype(BF16).reshape(right_ref.shape)

def attend(x, mask, gain1, wqkvg, gbias, wo, obias, gain2, wlr_t, first=0, count=4):
    groups, _, per, width = x.shape
    rows = groups * per
    whole = lambda a: pl.BlockSpec(a.shape, lambda k: (0,) * a.ndim)
    return pl.pallas_call(
        attend_kernel,
        grid=(count,),
        in_specs=[
            pl.BlockSpec((groups, 1, per, width), lambda k: (0, k + first, 0, 0)),
            pl.BlockSpec((1, 1, rows), lambda k: (k + first, 0, 0)),
            whole(gain1), whole(wqkvg), whole(gbias), whole(wo), whole(obias), whole(gain2), whole(wlr_t),
        ],
        out_specs=[
            pl.BlockSpec((1, rows, width), lambda k: (k, 0, 0)),
            pl.BlockSpec((1, 32, rows), lambda k: (k, 0, 0)),
            pl.BlockSpec((1, 32, rows), lambda k: (k, 0, 0)),
        ],
        out_shape=[
            jax.ShapeDtypeStruct((count, rows, width), BF16),
            jax.ShapeDtypeStruct((count, 32, rows), BF16),
            jax.ShapeDtypeStruct((count, 32, rows), BF16),
        ],
        scratch_shapes=[
            pltpu.VMEM((2, rows, 256), BF16),
            pltpu.VMEM((8, 256, rows), BF16),
            pltpu.VMEM((2, 4 * rows, 256), BF16),
            pltpu.VMEM((rows, 256), F32),
        ],
        compiler_params=pltpu.CompilerParams(vmem_limit_bytes=VMEM_LIMIT),
        cost_estimate=pl.CostEstimate(
            flops=count * 4 * 10**9, bytes_accessed=count * 10**6, transcendentals=count * 2 * 10**6
        ),
    )(x, mask, gain1, wqkvg, gbias, wo, obias, gain2, wlr_t)


def rearrange_kernel(order_ref, a_ref, b_ref, c_ref, out_ref, f_ref):
    pieces = [a_ref.at[0], a_ref.at[1], b_ref.at[0], b_ref.at[1]]
    pieces += [c_ref.at[n] for n in range(4)]
    for n in range(8):
        first = pl.multiple_of(order_ref[n] * 128, 128)
        r = pieces[n][...].reshape(128, 512).astype(F32)
        for c in range(4):
            f_ref[c, pl.ds(first, 128), :] = r[:, c * 128:(c + 1) * 128]
    for b in range(8):
        for c in range(4):
            part = jnp.concatenate(
                [f_ref[c, pl.ds(b * 4 + a, 32, stride=32), :] for a in range(4)], axis=0
            )
            out_ref[c * 128:(c + 1) * 128, b * 128:(b + 1) * 128] = part.astype(BF16).T


def rearrange(order, a, b, c):
    return pl.pallas_call(
        rearrange_kernel,
        in_specs=[pl.BlockSpec(memory_space=pltpu.SMEM)] + [pl.BlockSpec(memory_space=pltpu.VMEM)] * 3,
        out_shape=jax.ShapeDtypeStruct((512, 1024), BF16),
        scratch_shapes=[pltpu.VMEM((4, 1024, 128), F32)],
        compiler_params=pltpu.CompilerParams(vmem_limit_bytes=VMEM_LIMIT),
        cost_estimate=pl.CostEstimate(flops=10**6, bytes_accessed=4 * 10**6, transcendentals=0),
    )(order, a, b, c)


def pair_kernel(first, count, has_old, place_ref, *refs):
    parts = refs[:count]
    r_ref, w_ref, inv_ref, same_ref, bias_ref = refs[count:count + 5]
    out_ref, x_ref, y_ref, sems = refs[count + 5 + has_old:]
    copies = []
    halves = [(part, n) for part in parts for n in range(0, part.shape[0], 2)]

    def outer_product(part, n):
        return dot(part[n:n + 2].reshape(256, 512), r_ref[...]).astype(BF16)

    def project(at):
        y = dot(x_ref[(at // 2) % 2], w_ref[...])
        for n in range(8):
            lane = (first + at) * 4 + n
            scale = jnp.broadcast_to(inv_ref[:, lane:lane + 1], (32, 128))
            same = jnp.broadcast_to(same_ref[:, lane:lane + 1], (32, 128))
            result = y[n * 32:(n + 1) * 32] * scale + same * bias_ref[...]
            y_ref[at + n // 4, n % 4] = result.astype(BF16)
        for s in range(at, at + 2):
            copy = pltpu.make_async_copy(y_ref.at[s], out_ref.at[place_ref[first + s]], sems.at[s])
            copy.start()
            copies.append(copy)

    following = outer_product(*halves[0])
    for i in range(len(halves)):
        outer = following
        if i + 1 < len(halves):
            following = outer_product(*halves[i + 1])
        for n in range(8):
            a = jnp.concatenate(
                [outer[n * 32:(n + 1) * 32, b * 128:(b + 1) * 128] for b in range(8)], axis=0
            )
            t = a.T
            for q in range(4):
                x_ref[i % 2, n * 32:(n + 1) * 32, q * 256:(q + 1) * 256] = t[q * 32:(q + 1) * 32, :]
        if i:
            project(2 * i - 2)
    project(2 * len(halves) - 2)
    for copy in copies:
        copy.wait()


def pair(first, place, parts, r, w, inv, same, bias, old=None):
    count = len(parts)
    sources = sum(part.shape[0] for part in parts)
    vmem = pl.BlockSpec(memory_space=pltpu.VMEM)
    anywhere = pl.BlockSpec(memory_space=pl.ANY)
    has_old = old is not None
    return pl.pallas_call(
        functools.partial(pair_kernel, first, count, has_old),
        in_specs=[pl.BlockSpec(memory_space=pltpu.SMEM)] + [vmem] * (count + 5) + [anywhere] * has_old,
        out_specs=anywhere,
        out_shape=jax.ShapeDtypeStruct((32, 4, 32, 128), BF16),
        scratch_shapes=[
            pltpu.VMEM((2, 256, 1024), BF16),
            pltpu.VMEM((sources, 4, 32, 128), BF16),
            pltpu.SemaphoreType.DMA((sources,)),
        ],
        input_output_aliases={count + 6: 0} if has_old else {},
        compiler_params=pltpu.CompilerParams(vmem_limit_bytes=VMEM_LIMIT),
        cost_estimate=pl.CostEstimate(
            flops=sources * 25 * 10**7, bytes_accessed=sources * 4 * 10**5, transcendentals=0
        ),
    )(place, *parts, r, w, inv, same, bias, *([old] if has_old else []))


def coordinates(device):
    return [int(n) for n in np.unravel_index(device, (4, 2, 4, 2, 4))]


def permute_all(value, move):
    pairs = []
    for source in range(256):
        pairs.append((source, int(np.ravel_multi_index(move(*coordinates(source)), (4, 2, 4, 2, 4)))))
    return lax.ppermute(value, ("row", "col"), pairs)


def shifted(phase, shift):
    def move(zl, co, x, zh, y):
        if (co + phase) % 2 == 0:
            return zl, co, x, zh, (y + shift) % 4
        return zl, co, (x + shift) % 4, zh, y

    return move


SHIFTS = (0, 1, 3, 2)


def after(value, *others):
    anywhere = pl.BlockSpec(memory_space=pl.ANY)

    def nothing(*refs):
        pass

    return pl.pallas_call(
        nothing,
        in_specs=[anywhere] * (1 + len(others)),
        out_specs=anywhere,
        out_shape=jax.ShapeDtypeStruct(value.shape, value.dtype),
        input_output_aliases={0: 0},
        cost_estimate=pl.CostEstimate(flops=0, bytes_accessed=0, transcendentals=0),
    )(value, *others)


def body(
    alignment, column_mask, chain_index, attention_norm_gain, query_weight, key_weight, value_matrix,
    gate_matrix, gate_bias, attention_output_weight, attention_output_bias, outer_norm_gain,
    left_factor_weight, right_factor_weight, pair_weight, chain_bias,
):
    row = lax.axis_index("row")
    col = lax.axis_index("col")
    z_lo, core = row // 2, row % 2
    x, z_hi, y = col // 8, (col // 4) % 2, col % 4
    moved = alignment.reshape(16, 32, 4, 256).transpose(1, 2, 0, 3)
    regrouped = lax.all_to_all(moved, "col", split_axis=0, concat_axis=0, tiled=True)

    place = []
    for s in SHIFTS:
        for t in SHIFTS:
            for z in range(2):
                by_y = ((x - s) % 4) * 8 + (z_hi ^ z) * 4 + (y - t) % 4
                by_x = ((x - t) % 4) * 8 + (z_hi ^ z) * 4 + (y - s) % 4
                place.append(jnp.where(core == 0, by_y, by_x))
    place = jnp.stack(place).astype(jnp.int32)
    order = jnp.stack(
        [(core ^ c) * 4 + (z_lo ^ n) for c in range(2) for n in (0, 2, 1, 3)]
    ).astype(jnp.int32)

    own_mask = lax.dynamic_slice_in_dim(column_mask, row * 128 + col * 4, 4, 1).T
    live = own_mask.astype(F32).reshape(4, 1, 512)
    row_mask = lax.dynamic_slice_in_dim(column_mask, row * 128, 128, 1).astype(BF16)
    col_mask = lax.dynamic_slice_in_dim(column_mask, col * 32, 32, 1).astype(BF16)
    counts = lax.dot_general(col_mask, row_mask, (((0,), (0,)), ((), ())), preferred_element_type=F32)
    row_chain = lax.dynamic_slice_in_dim(chain_index, row * 128, 128, 0)
    col_chain = lax.dynamic_slice_in_dim(chain_index, col * 32, 32, 0)
    same = (col_chain[:, None] == row_chain[None, :]).astype(F32)
    residue = (place[:, None] * 4 + jnp.arange(4)[None, :]).reshape(128)
    chosen = (jnp.arange(128)[:, None] == residue[None, :]).astype(F32)
    arrived = jnp.dot(jnp.concatenate([1.0 / (counts + 0.001), same]), chosen, precision=lax.Precision.HIGHEST)
    inverse, same = arrived[:32], arrived[32:]
    wqkvg = jnp.concatenate([query_weight, key_weight, value_matrix, gate_matrix], axis=1)
    wlr = jnp.concatenate([left_factor_weight, right_factor_weight], axis=1).T
    wpair = pair_weight.reshape(32, 8, 4, 128).transpose(2, 1, 0, 3).reshape(1024, 128)
    prepared = (live, wqkvg, wlr, wpair, inverse, same, place, order)
    regrouped, prepared = lax.optimization_barrier((regrouped, prepared))
    live, wqkvg, wlr, wpair, inverse, same, place, order = prepared

    up, left, right = attend(
        regrouped, live, attention_norm_gain[None], wqkvg, gate_bias[None],
        attention_output_weight, attention_output_bias[None], outer_norm_gain[None], wlr,
    )
    updated = up.transpose(1, 0, 2)

    beside = permute_all(left, lambda zl, co, x, zh, y: (zl, co, x, 1 - zh, y))
    near = permute_all(right, lambda zl, co, x, zh, y: (y, zh, zl, co, x))
    far = permute_all(after(right, beside), lambda zl, co, x, zh, y: (y ^ 2, zh, zl, co, x))
    own = jnp.stack([left, beside])
    line = jnp.concatenate([own] + [permute_all(own, shifted(0, s)) for s in SHIFTS[1:]])
    right_a = jnp.stack([near, far])
    right_b = permute_all(right_a, lambda zl, co, x, zh, y: (zl ^ 1, co, x, zh, y))
    below, above = permute_all(line, shifted(1, 1)), permute_all(line, shifted(1, 3))
    parts = [line, below, above, permute_all(below[:4], shifted(1, 1)), permute_all(above[4:], shifted(1, 3))]
    right_c = permute_all(
        after(jnp.concatenate([right_a, right_b]), updated), lambda zl, co, x, zh, y: (zl, 1 - co, x, zh, y)
    )
    r = rearrange(order, right_a, right_b, right_c)
    out = None
    for first, some in ((0, parts[:3]), (24, parts[3:])):
        out = pair(first, place, some, r, wpair, inverse, same, chain_bias[None], out)
    return updated, out.reshape(128, 32, 128)


def solution(mesh):
    return jax.shard_map(
        body,
        mesh=mesh,
        in_specs=(P("col", "row", None),) + (P(),) * 15,
        out_specs=(P(None, ("row", "col"), None), P("row", "col", None)),
        check_vma=False,
    )
```

```python
import functools
import math

import jax
import jax.numpy as jnp
import numpy as np
from jax import lax
from jax.experimental import pallas as pl
from jax.experimental.pallas import tpu as pltpu
from jax.sharding import PartitionSpec as P

HEAD_FEATURES = 32
F32, BF16 = jnp.float32, jnp.bfloat16
SB = 128
VMEM_LIMIT = 40 * 1024 * 1024

def norm_rows(x, gain):
    average = jnp.mean(x, -1, keepdims=True)
    centred = x - average
    variance = jnp.mean(centred * centred, -1, keepdims=True)
    return centred * lax.rsqrt(variance + 1e-05) * gain

def dot(a, b):
    return jnp.dot(a, b, preferred_element_type=F32)

def dot_nt(a, b):
    return lax.dot_general(a, b, (((1,), (1,)), ((), ())), preferred_element_type=F32)

def attend_kernel(
    parts_ref, mask_ref, gain1_ref, wqkvg_ref, gbias_ref, wo_ref, obias_ref, gain2_ref, wlr_ref,
    up_ref, left_ref, right_ref, qa_ref, ka_ref, va_ref, gated_ref,
):
    rows = qa_ref.shape[1]
    lane = lax.broadcasted_iota(jnp.int32, (1, 128), 1)

    @pl.when(pl.program_id(0) == 0)
    def _():
        ka_ref[...] = jnp.zeros_like(ka_ref)
        ones = jnp.broadcast_to(jnp.where(lane == 0, 1.0, 0.0).astype(BF16), (rows, 128))
        for g in range(2):
            qa_ref[g, :, 128:] = ones
            for h in range(4):
                va_ref[g, h * rows:(h + 1) * rows, 128:] = jnp.broadcast_to(
                    jnp.where(lane // 32 == h, 1.0, 0.0).astype(BF16), (rows, 128))

    x = parts_ref[...].reshape(rows, 256).astype(F32)
    normed = norm_rows(x, gain1_ref[...]).astype(BF16)
    scale = math.log2(math.e) * HEAD_FEATURES ** (-0.5)
    queries = (dot(normed, wqkvg_ref[:, 0:256]) * scale).astype(BF16)
    keys = dot(normed, wqkvg_ref[:, 256:512]).astype(BF16).T
    values = dot(normed, wqkvg_ref[:, 512:768]).astype(BF16)
    live = mask_ref[...].reshape(1, rows)
    dead = jnp.where(lax.broadcasted_iota(jnp.int32, (16, 1), 0) == 0, (live - 1.0) * 1e9, 0.0).astype(BF16)
    for g in range(2):
        qa_ref[g, :, :128] = queries[:, g * 128:(g + 1) * 128]
        for h in range(4):
            n = g * 4 + h
            ka_ref[n, h * 32:(h + 1) * 32, :] = keys[n * 32:(n + 1) * 32, :]
            ka_ref[n, 128:144, :] = dead
            kept = jnp.where(lane // 32 == h, 1.0, 0.0).astype(BF16)
            va_ref[g, h * rows:(h + 1) * rows, :128] = values[:, g * 128:(g + 1) * 128] * kept
    gated_ref[...] = jax.nn.sigmoid(dot(normed, wqkvg_ref[:, 768:1024]) + gbias_ref[...])
    for g in range(2):
        for b in range(rows // SB):
            q = qa_ref[g, b * SB:(b + 1) * SB, :]
            total = None
            for h in range(4):
                s = dot(q, ka_ref[g * 4 + h])
                m = jnp.max(s, axis=-1, keepdims=True)
                p = jnp.exp2(s - m).astype(BF16)
                part = dot(p, va_ref[g, h * rows:(h + 1) * rows, :])
                total = part if total is None else total + part
            out = total[:, :128] / total[:, 128:]
            sl = (slice(b * SB, (b + 1) * SB), slice(g * 128, (g + 1) * 128))
            gated_ref[sl] = gated_ref[sl] * out
    gated = gated_ref[...].astype(BF16)
    updated = (dot(gated, wo_ref[...]) + obias_ref[...] + x).astype(BF16)
    up_ref[...] = updated.reshape(up_ref.shape)
    again = norm_rows(updated.astype(F32), gain2_ref[...]).astype(BF16)
    factors = dot_nt(wlr_ref[...], again) * live
    left_ref[...] = factors[:32].astype(BF16).reshape(left_ref.shape)
    right_ref[...] = factors[32:].astype(BF16).reshape(right_ref.shape)

def attend(x, mask, gain1, wqkvg, gbias, wo, obias, gain2, wlr_t, first=0, count=4):
    groups, _, per, width = x.shape
    rows = groups * per
    whole = lambda a: pl.BlockSpec(a.shape, lambda k: (0,) * a.ndim)
    return pl.pallas_call(
        attend_kernel,
        grid=(count,),
        in_specs=[
            pl.BlockSpec((groups, 1, per, width), lambda k: (0, k + first, 0, 0)),
            pl.BlockSpec((1, 1, rows), lambda k: (k + first, 0, 0)),
            whole(gain1), whole(wqkvg), whole(gbias), whole(wo), whole(obias), whole(gain2), whole(wlr_t),
        ],
        out_specs=[
            pl.BlockSpec((1, rows, width), lambda k: (k, 0, 0)),
            pl.BlockSpec((1, 32, rows), lambda k: (k, 0, 0)),
            pl.BlockSpec((1, 32, rows), lambda k: (k, 0, 0)),
        ],
        out_shape=[
            jax.ShapeDtypeStruct((count, rows, width), BF16),
            jax.ShapeDtypeStruct((count, 32, rows), BF16),
            jax.ShapeDtypeStruct((count, 32, rows), BF16),
        ],
        scratch_shapes=[
            pltpu.VMEM((2, rows, 256), BF16),
            pltpu.VMEM((8, 256, rows), BF16),
            pltpu.VMEM((2, 4 * rows, 256), BF16),
            pltpu.VMEM((rows, 256), F32),
        ],
        compiler_params=pltpu.CompilerParams(vmem_limit_bytes=VMEM_LIMIT),
        cost_estimate=pl.CostEstimate(
            flops=count * 4 * 10**9, bytes_accessed=count * 10**6, transcendentals=count * 2 * 10**6
        ),
    )(x, mask, gain1, wqkvg, gbias, wo, obias, gain2, wlr_t)


def rearrange_kernel(order_ref, a_ref, b_ref, c_ref, out_ref, f_ref):
    pieces = [a_ref.at[0], a_ref.at[1], b_ref.at[0], b_ref.at[1]]
    pieces += [c_ref.at[n] for n in range(4)]
    for n in range(8):
        first = pl.multiple_of(order_ref[n] * 128, 128)
        r = pieces[n][...].reshape(128, 512).astype(F32)
        for c in range(4):
            f_ref[c, pl.ds(first, 128), :] = r[:, c * 128:(c + 1) * 128]
    for b in range(8):
        for c in range(4):
            part = jnp.concatenate(
                [f_ref[c, pl.ds(b * 4 + a, 32, stride=32), :] for a in range(4)], axis=0
            )
            out_ref[c * 128:(c + 1) * 128, b * 128:(b + 1) * 128] = part.astype(BF16).T


def rearrange(order, a, b, c):
    return pl.pallas_call(
        rearrange_kernel,
        in_specs=[pl.BlockSpec(memory_space=pltpu.SMEM)] + [pl.BlockSpec(memory_space=pltpu.VMEM)] * 3,
        out_shape=jax.ShapeDtypeStruct((512, 1024), BF16),
        scratch_shapes=[pltpu.VMEM((4, 1024, 128), F32)],
        compiler_params=pltpu.CompilerParams(vmem_limit_bytes=VMEM_LIMIT),
        cost_estimate=pl.CostEstimate(flops=10**6, bytes_accessed=4 * 10**6, transcendentals=0),
    )(order, a, b, c)


def pair_kernel(first, count, has_old, place_ref, *refs):
    parts = refs[:count]
    r_ref, w_ref, inv_ref, same_ref, bias_ref = refs[count:count + 5]
    out_ref, x_ref, y_ref, sems = refs[count + 5 + has_old:]
    copies = []
    halves = [(part, n) for part in parts for n in range(0, part.shape[0], 2)]

    def outer_product(part, n):
        return dot(part[n:n + 2].reshape(256, 512), r_ref[...]).astype(BF16)

    def project(at):
        y = dot(x_ref[(at // 2) % 2], w_ref[...])
        for n in range(8):
            lane = (first + at) * 4 + n
            scale = jnp.broadcast_to(inv_ref[:, lane:lane + 1], (32, 128))
            same = jnp.broadcast_to(same_ref[:, lane:lane + 1], (32, 128))
            result = y[n * 32:(n + 1) * 32] * scale + same * bias_ref[...]
            y_ref[at + n // 4, n % 4] = result.astype(BF16)
        for s in range(at, at + 2):
            copy = pltpu.make_async_copy(y_ref.at[s], out_ref.at[place_ref[first + s]], sems.at[s])
            copy.start()
            copies.append(copy)

    following = outer_product(*halves[0])
    for i in range(len(halves)):
        outer = following
        if i + 1 < len(halves):
            following = outer_product(*halves[i + 1])
        for n in range(8):
            a = jnp.concatenate(
                [outer[n * 32:(n + 1) * 32, b * 128:(b + 1) * 128] for b in range(8)], axis=0
            )
            t = a.T
            for q in range(4):
                x_ref[i % 2, n * 32:(n + 1) * 32, q * 256:(q + 1) * 256] = t[q * 32:(q + 1) * 32, :]
        if i:
            project(2 * i - 2)
    project(2 * len(halves) - 2)
    for copy in copies:
        copy.wait()


def pair(first, place, parts, r, w, inv, same, bias, old=None):
    count = len(parts)
    sources = sum(part.shape[0] for part in parts)
    vmem = pl.BlockSpec(memory_space=pltpu.VMEM)
    anywhere = pl.BlockSpec(memory_space=pl.ANY)
    has_old = old is not None
    return pl.pallas_call(
        functools.partial(pair_kernel, first, count, has_old),
        in_specs=[pl.BlockSpec(memory_space=pltpu.SMEM)] + [vmem] * (count + 5) + [anywhere] * has_old,
        out_specs=anywhere,
        out_shape=jax.ShapeDtypeStruct((32, 4, 32, 128), BF16),
        scratch_shapes=[
            pltpu.VMEM((2, 256, 1024), BF16),
            pltpu.VMEM((sources, 4, 32, 128), BF16),
            pltpu.SemaphoreType.DMA((sources,)),
        ],
        input_output_aliases={count + 6: 0} if has_old else {},
        compiler_params=pltpu.CompilerParams(vmem_limit_bytes=VMEM_LIMIT),
        cost_estimate=pl.CostEstimate(
            flops=sources * 25 * 10**7, bytes_accessed=sources * 4 * 10**5, transcendentals=0
        ),
    )(place, *parts, r, w, inv, same, bias, *([old] if has_old else []))


def coordinates(device):
    return [int(n) for n in np.unravel_index(device, (4, 2, 4, 2, 4))]


def permute_all(value, move):
    pairs = []
    for source in range(256):
        pairs.append((source, int(np.ravel_multi_index(move(*coordinates(source)), (4, 2, 4, 2, 4)))))
    return lax.ppermute(value, ("row", "col"), pairs)


def shifted(phase, shift):
    def move(zl, co, x, zh, y):
        if (co + phase) % 2 == 0:
            return zl, co, x, zh, (y + shift) % 4
        return zl, co, (x + shift) % 4, zh, y

    return move


SHIFTS = (0, 1, 3, 2)


def after(value, *others):
    anywhere = pl.BlockSpec(memory_space=pl.ANY)

    def nothing(*refs):
        pass

    return pl.pallas_call(
        nothing,
        in_specs=[anywhere] * (1 + len(others)),
        out_specs=anywhere,
        out_shape=jax.ShapeDtypeStruct(value.shape, value.dtype),
        input_output_aliases={0: 0},
        cost_estimate=pl.CostEstimate(flops=0, bytes_accessed=0, transcendentals=0),
    )(value, *others)


def body(
    alignment, column_mask, chain_index, attention_norm_gain, query_weight, key_weight, value_matrix,
    gate_matrix, gate_bias, attention_output_weight, attention_output_bias, outer_norm_gain,
    left_factor_weight, right_factor_weight, pair_weight, chain_bias,
):
    row = lax.axis_index("row")
    col = lax.axis_index("col")
    z_lo, core = row // 2, row % 2
    x, z_hi, y = col // 8, (col // 4) % 2, col % 4
    moved = alignment.reshape(16, 32, 4, 256).transpose(1, 2, 0, 3)
    regrouped = lax.all_to_all(moved, "col", split_axis=0, concat_axis=0, tiled=True)

    place = []
    for s in SHIFTS:
        for t in SHIFTS:
            for z in range(2):
                by_y = ((x - s) % 4) * 8 + (z_hi ^ z) * 4 + (y - t) % 4
                by_x = ((x - t) % 4) * 8 + (z_hi ^ z) * 4 + (y - s) % 4
                place.append(jnp.where(core == 0, by_y, by_x))
    place = jnp.stack(place).astype(jnp.int32)
    order = jnp.stack(
        [(core ^ c) * 4 + (z_lo ^ n) for c in range(2) for n in (0, 2, 1, 3)]
    ).astype(jnp.int32)

    own_mask = lax.dynamic_slice_in_dim(column_mask, row * 128 + col * 4, 4, 1).T
    live = own_mask.astype(F32).reshape(4, 1, 512)
    row_mask = lax.dynamic_slice_in_dim(column_mask, row * 128, 128, 1).astype(BF16)
    col_mask = lax.dynamic_slice_in_dim(column_mask, col * 32, 32, 1).astype(BF16)
    counts = lax.dot_general(col_mask, row_mask, (((0,), (0,)), ((), ())), preferred_element_type=F32)
    row_chain = lax.dynamic_slice_in_dim(chain_index, row * 128, 128, 0)
    col_chain = lax.dynamic_slice_in_dim(chain_index, col * 32, 32, 0)
    same = (col_chain[:, None] == row_chain[None, :]).astype(F32)
    residue = (place[:, None] * 4 + jnp.arange(4)[None, :]).reshape(128)
    chosen = (jnp.arange(128)[:, None] == residue[None, :]).astype(F32)
    arrived = jnp.dot(jnp.concatenate([1.0 / (counts + 0.001), same]), chosen, precision=lax.Precision.HIGHEST)
    inverse, same = arrived[:32], arrived[32:]
    wqkvg = jnp.concatenate([query_weight, key_weight, value_matrix, gate_matrix], axis=1)
    wlr = jnp.concatenate([left_factor_weight, right_factor_weight], axis=1).T
    wpair = pair_weight.reshape(32, 8, 4, 128).transpose(2, 1, 0, 3).reshape(1024, 128)
    prepared = (live, wqkvg, wlr, wpair, inverse, same, place, order)
    regrouped, prepared = lax.optimization_barrier((regrouped, prepared))
    live, wqkvg, wlr, wpair, inverse, same, place, order = prepared

    up, left, right = attend(
        regrouped, live, attention_norm_gain[None], wqkvg, gate_bias[None],
        attention_output_weight, attention_output_bias[None], outer_norm_gain[None], wlr,
    )
    updated = up.transpose(1, 0, 2)

    beside = permute_all(left, lambda zl, co, x, zh, y: (zl, co, x, 1 - zh, y))
    near = permute_all(right, lambda zl, co, x, zh, y: (y, zh, zl, co, x))
    far = permute_all(after(right, beside), lambda zl, co, x, zh, y: (y ^ 2, zh, zl, co, x))
    own = jnp.stack([left, beside])
    line = jnp.concatenate([own] + [permute_all(own, shifted(0, s)) for s in SHIFTS[1:]])
    right_a = jnp.stack([near, far])
    right_b = permute_all(right_a, lambda zl, co, x, zh, y: (zl ^ 1, co, x, zh, y))
    below, above = permute_all(line, shifted(1, 1)), permute_all(line, shifted(1, 3))
    parts = [line, below, above, permute_all(below[:4], shifted(1, 1)), permute_all(above[4:], shifted(1, 3))]
    right_c = permute_all(
        after(jnp.concatenate([right_a, right_b]), updated), lambda zl, co, x, zh, y: (zl, 1 - co, x, zh, y)
    )
    r = rearrange(order, right_a, right_b, right_c)
    out = None
    for first, some in ((0, parts[:3]), (24, parts[3:])):
        out = pair(first, place, some, r, wpair, inverse, same, chain_bias[None], out)
    return updated, out.reshape(128, 32, 128)


def solution(mesh):
    return jax.shard_map(
        body,
        mesh=mesh,
        in_specs=(P("col", "row", None),) + (P(),) * 15,
        out_specs=(P(None, ("row", "col"), None), P("row", "col", None)),
        check_vma=False,
    )
```
